32 devices in a mesh: groups: 2 (over x), band: 8 (over z, y), col: 2 (over core).
Axes of the slice: x: 2, y: 2, z: 4, core: 2. Of those that a mesh axis runs over, the one named last changes fastest.
Arguments:
- row_inputs: float32 [8192, 64], P(('groups', 'band', 'col')), parts along dimension 0, may hold values from 0.05 to 0.95
- col_inputs: float32 [65536, 64], P(('groups', 'band', 'col')), parts along dimension 0, may hold values from 0.05 to 0.95
- row_factors: float32 [8192, 66], P(('groups', 'band', 'col')), parts along dimension 0, may hold values from -0.75 to 0.75
- col_factors: float32 [65536, 66], P(('groups', 'band', 'col')), parts along dimension 0, may hold values from -0.44595265 to 0.44595265
- warp_a: float32 [128], P('groups'), parts along dimension 0, may hold values from 0.5 to 2
- warp_b: float32 [128], P('groups'), parts along dimension 0, may hold values from 0.5 to 2
- lengthscale: float32 [128], P('groups'), parts along dimension 0, may hold values from 1 to 4
Outputs:
- row_grad: float32 [8192, 64], P(('groups', 'band', 'col')), parts along dimension 0
- col_grad: float32 [65536, 64], P(('groups', 'band', 'col')), parts along dimension 0
The draws below stay inside these ranges and needn't reach their ends.
There are 2 independent parts, one for each index of `groups`. The reference program is written for one: setup_inputs(seed, part) draws one part's arguments, and reference() takes and returns one part's arrays. A program takes and returns all parts, laid end to end along the dimension named above; each array names one. Nothing has to cross between parts.
All inputs are finite; a program needn't handle non-finite values.
Results may differ from the reference program's by a relative error of at most 0.00016.
Values sent between devices are 32-bit elements; how exact they have to be, the bound alone decides.
A program may use at most 128 MiB of HBM per device.

```python
import math
import jax
import jax.numpy as jnp
from jax import lax

KNOBS = 64
RANK = 33
ROWS = 4096
COLS = 32768


def shard_levels(stream_key, shape, shards, low, top_value):
    gain = 1.0
    for position, shards_of in shards:
        draws = jax.random.uniform(jax.random.fold_in(jax.random.fold_in(stream_key, 6), position), (shards_of,), jnp.float32, low / len(shards), top_value / len(shards))
        gain = gain * jnp.repeat(jnp.exp(draws), shape[position] // shards_of).reshape((-1,) + (1,) * (len(shape) - 1 - position))
    return gain


def normal_values(stream_key, shape, spread, reach, pieces=(), kind=jnp.bfloat16):
    values = spread * jax.random.normal(stream_key, shape, jnp.float32)
    if pieces:
        values = values * shard_levels(stream_key, shape, pieces, -0.22, 0.18)
    return jnp.clip(values, -reach, reach).astype(kind)


def setup_inputs(seed: int = 0, part: int = 0) -> dict:
    splits = jax.random.split(jax.random.key(seed), 8)
    part_keys = jax.random.split(jax.random.fold_in(splits[7], part), 8)
    return {
        "row_inputs": jnp.clip(0.05 + 0.9 * jax.random.uniform(part_keys[0], (ROWS, KNOBS), jnp.float32) ** shard_levels(part_keys[0], (ROWS, KNOBS), ((0, 16),), -0.2, 0.2), 0.05, 0.95),
        "col_inputs": jnp.clip(0.05 + 0.9 * jax.random.uniform(part_keys[1], (COLS, KNOBS), jnp.float32) ** shard_levels(part_keys[1], (COLS, KNOBS), ((0, 16),), -0.2, 0.2), 0.05, 0.95),
        "row_factors": normal_values(part_keys[2], (ROWS, 2 * RANK), (ROWS ** -0.25), 0.75, ((0, 16),), jnp.float32),
        "col_factors": normal_values(part_keys[3], (COLS, 2 * RANK), (COLS ** -0.25), 0.44595265, ((0, 16),), jnp.float32),
        "warp_a": jnp.clip(jnp.exp(jax.random.uniform(part_keys[4], (KNOBS,), jnp.float32, math.log(0.5), math.log(2.0))), 0.5, 2.0),
        "warp_b": jnp.clip(jnp.exp(jax.random.uniform(part_keys[5], (KNOBS,), jnp.float32, math.log(0.5), math.log(2.0))), 0.5, 2.0),
        "lengthscale": jnp.clip(jnp.exp(jax.random.uniform(part_keys[6], (KNOBS,), jnp.float32, math.log(1.0), math.log(4.0))), 1.0, 4.0),
    }


precise_mode = lax.Precision.HIGHEST


def warped(inputs, warp_a, warp_b, lengthscale):
    powered = inputs ** warp_a
    coords = (1.0 - (1.0 - powered) ** warp_b) / lengthscale
    slope = warp_a * warp_b * inputs ** (warp_a - 1.0) * (1.0 - powered) ** (warp_b - 1.0) / lengthscale
    return coords, slope


def swapped(factors):
    half_width = factors.shape[1] // 2
    return jnp.concatenate([factors[:, half_width:], factors[:, :half_width]], axis=1)


def tile_terms(row_coords, row_mix, col_coords, col_mix):
    inner_prod = jnp.dot(row_coords, col_coords.T, precision=precise_mode)
    row_norms = jnp.sum(row_coords * row_coords, axis=1)
    col_norms = jnp.sum(col_coords * col_coords, axis=1)
    distance = row_norms[:, None] + col_norms[None, :] - 2.0 * inner_prod
    kernel = jnp.exp(-0.5 * distance)
    weights = jnp.dot(row_mix, col_mix.T, precision=precise_mode) * kernel
    row_part = jnp.dot(weights, col_coords, precision=precise_mode)
    col_part = jnp.dot(weights.T, row_coords, precision=precise_mode)
    return row_part, jnp.sum(weights, axis=1), col_part, jnp.sum(weights, axis=0)


def reference(row_inputs, col_inputs, row_factors, col_factors, warp_a, warp_b, lengthscale):
    row_coords, row_slope = warped(row_inputs, warp_a, warp_b, lengthscale)
    col_coords, col_slope = warped(col_inputs, warp_a, warp_b, lengthscale)
    col_mix = swapped(col_factors)
    block_size = math.gcd(COLS, 4096)
    count = COLS // block_size

    def visit_block(carried, columns):
        row_part, row_total, col_part, col_total = tile_terms(row_coords, row_factors, columns[0], columns[1])
        return (carried[0] + row_part, carried[1] + row_total), (col_part, col_total)

    initial = (jnp.zeros((ROWS, KNOBS), jnp.float32), jnp.zeros((ROWS,), jnp.float32))
    (row_pull, row_total), (col_pull, col_total) = lax.scan(
        visit_block, initial,
        (col_coords.reshape(count, block_size, KNOBS), col_mix.reshape(count, block_size, 2 * RANK)))
    col_pull = col_pull.reshape(COLS, KNOBS)
    col_total = col_total.reshape(COLS)
    row_grad = (row_pull - row_total[:, None] * row_coords) * row_slope
    col_grad = (col_pull - col_total[:, None] * col_coords) * col_slope
    return row_grad, col_grad
```

```python
import functools
import math

import jax
import jax.numpy as jnp
from jax import lax
from jax.experimental import pallas as pl
from jax.experimental.pallas import tpu as pltpu
from jax.sharding import PartitionSpec as P

LOG2E = math.log2(math.e)
TILE = 256


def up(value, multiple):
    return -(-value // multiple) * multiple


def warped_t(inputs, warp_a, warp_b, lengthscale):
    powered = jnp.exp(warp_a * jnp.log(inputs))
    rest = 1.0 - powered
    rest_b = jnp.exp(warp_b * jnp.log(rest))
    coords = (0.5 - rest_b) / lengthscale
    slope = warp_a * warp_b * powered * rest_b / (inputs * rest * lengthscale)
    return coords, slope


def high(values):
    return values.astype(jnp.bfloat16).astype(jnp.float32)


def norm_rows(values, scale, first):
    norm = scale * jnp.sum(values * values, axis=0, keepdims=True)
    top = high(norm)
    middle = high(norm - top)
    last = norm - top - middle
    index = lax.broadcasted_iota(jnp.int32, (8, values.shape[1]), 0) - first
    ones = lax.broadcasted_iota(jnp.int32, (8, values.shape[1]), 0) - (3 - first)
    rows = jnp.where((ones >= 0) & (ones < 3), 1.0, 0.0)
    rows = jnp.where(index == 0, top, rows)
    rows = jnp.where(index == 1, middle, rows)
    return jnp.where(index == 2, last, rows)


def stacked(parts, depth):
    width = parts[0].shape[1]
    have = sum(part.shape[0] for part in parts)
    if depth > have:
        parts = parts + [jnp.zeros((depth - have, width), jnp.float32)]
    return jnp.concatenate(parts, axis=0).astype(jnp.bfloat16)


def pull_rows(coords):
    top = high(coords)
    index = lax.broadcasted_iota(jnp.int32, (16, coords.shape[1]), 0)
    return stacked([top, jnp.where(index == 0, 1.0, 0.0), coords - top], 2 * coords.shape[0] + 16)


def packed_rows(inputs, factors, warp_a, warp_b, lengthscale):
    coords, _ = warped_t(inputs.T, warp_a, warp_b, lengthscale)
    mix = factors.T
    pad = up(mix.shape[0], 8) - mix.shape[0]
    if pad:
        mix = jnp.concatenate([mix, jnp.zeros((pad, mix.shape[1]), jnp.float32)], axis=0)
    return jnp.concatenate([coords, mix], axis=0)


def prepare_cols(sizes, col_inputs, col_factors, params, dist_b, mix_b, col_pull):
    knobs, half, mixes = sizes
    for start in range(0, col_inputs.shape[0], TILE):
        here = pl.ds(start, TILE)
        coords, _ = warped_t(col_inputs[here, :].T, *params)
        scaled = coords * LOG2E
        top = high(scaled)
        dist_b[:, here] = stacked(
            [top, scaled - top, top, norm_rows(coords, -0.5 * LOG2E, 3)], dist_b.shape[0]
        )
        mix = col_factors[here, :].T
        mix = jnp.concatenate(
            [mix[half:], mix[:half], jnp.zeros((mixes - 2 * half, TILE), jnp.float32)], axis=0
        )
        top = high(mix)
        mix_b[:, here] = stacked([top, mix - top, top], mix_b.shape[0])
        col_pull[:, here] = pull_rows(coords)


def process_block(sizes, packed, dist_b, mix_b, col_pull, col_acc):
    knobs, half, mixes = sizes
    coords, mix = packed[:knobs], packed[knobs:]
    top = high(coords)
    dist_a = stacked(
        [top, top, coords - top, norm_rows(coords, -0.5 * LOG2E, 0)], dist_b.shape[0]
    ).T
    top = high(mix)
    mix_a = stacked([top, top, mix - top], mix_b.shape[0]).T
    row_pull = pull_rows(coords)
    lead = knobs + 16
    part = jnp.zeros((row_pull.shape[0], packed.shape[1]), jnp.float32)
    part_low = jnp.zeros((lead, packed.shape[1]), jnp.float32)
    nt = (((1,), (1,)), ((), ()))
    for start in range(0, dist_b.shape[1], TILE):
        here = pl.ds(start, TILE)
        power = jnp.dot(dist_a, dist_b[:, here], preferred_element_type=jnp.float32)
        inner = jnp.dot(mix_a, mix_b[:, here], preferred_element_type=jnp.float32)
        weights = inner * jnp.exp2(power)
        top = weights.astype(jnp.bfloat16)
        low = (weights - top.astype(jnp.float32)).astype(jnp.bfloat16)
        part += lax.dot_general(col_pull[:, here], top, nt, preferred_element_type=jnp.float32)
        part_low += lax.dot_general(col_pull[:lead, here], low, nt, preferred_element_type=jnp.float32)
        col_acc[:lead, here] += jnp.dot(
            row_pull[:lead], top, preferred_element_type=jnp.float32
        ) + jnp.dot(row_pull[:lead], low, preferred_element_type=jnp.float32)
        col_acc[lead:, here] += jnp.dot(row_pull[lead:], top, preferred_element_type=jnp.float32)
    pulled = part[:knobs] + part_low[:knobs] + part[lead:]
    return jnp.concatenate([pulled, part[knobs : knobs + 8] + part_low[knobs : knobs + 8]], axis=0)


def finish_cols(sizes, col_inputs, params, col_acc, col_grad):
    knobs, half, mixes = sizes
    lead = knobs + 16
    for start in range(0, col_inputs.shape[0], TILE):
        here = pl.ds(start, TILE)
        coords, slope = warped_t(col_inputs[here, :].T, *params)
        pulled = col_acc[:knobs, here] + col_acc[lead:, here]
        total = col_acc[knobs : knobs + 1, here]
        col_grad[here, :] = ((pulled - total * coords) * slope).T


def local_kernel(
    sizes, rows_ref, col_inputs, col_factors, params_ref, parts, col_grad, dist_b, mix_b, col_pull, col_acc
):
    params = (params_ref[:, 0:1], params_ref[:, 1:2], params_ref[:, 2:3])
    prepare_cols(sizes, col_inputs, col_factors, params, dist_b, mix_b, col_pull)
    col_acc[...] = jnp.zeros_like(col_acc)

    def step(block, carry):
        parts[block] = process_block(sizes, rows_ref[block], dist_b, mix_b, col_pull, col_acc)
        return carry

    lax.fori_loop(0, rows_ref.shape[0], step, 0)
    finish_cols(sizes, col_inputs, params, col_acc, col_grad)


def on_device(row_inputs, col_inputs, row_factors, col_factors, warp_a, warp_b, lengthscale):
    knobs = row_inputs.shape[1]
    rows, cols = row_inputs.shape[0], col_inputs.shape[0]
    half = row_factors.shape[1] // 2
    mixes = up(2 * half, 8)
    sizes = (knobs, half, mixes)
    params = jnp.stack([warp_a, warp_b, lengthscale], axis=1)
    columns = (params[:, 0:1], params[:, 1:2], params[:, 2:3])
    packed = packed_rows(row_inputs, row_factors, *columns)
    gathered = lax.all_gather(packed, ("band", "col"), axis=0)
    blocks = gathered.shape[0]
    parts, col_grad = pl.pallas_call(
        functools.partial(local_kernel, sizes),
        out_shape=(
            jax.ShapeDtypeStruct((blocks, knobs + 8, rows), jnp.float32),
            jax.ShapeDtypeStruct((cols, knobs), jnp.float32),
        ),
        in_specs=[pl.BlockSpec(memory_space=pltpu.VMEM)] * 4,
        out_specs=[pl.BlockSpec(memory_space=pltpu.VMEM)] * 2,
        scratch_shapes=[
            pltpu.VMEM((up(3 * knobs + 8, 256), cols), jnp.bfloat16),
            pltpu.VMEM((up(3 * mixes, 256), cols), jnp.bfloat16),
            pltpu.VMEM((2 * knobs + 16, cols), jnp.bfloat16),
            pltpu.VMEM((2 * knobs + 16, cols), jnp.float32),
        ],
        compiler_params=pltpu.CompilerParams(vmem_limit_bytes=40 * 1024 * 1024),
        name="local_pairs",
    )(gathered, col_inputs, col_factors, params)
    mine = lax.psum_scatter(parts, ("band", "col"), scatter_dimension=0)
    coords, slope = warped_t(row_inputs.T, *columns)
    row_grad = ((mine[:knobs] - mine[knobs : knobs + 1] * coords) * slope).T
    return row_grad, col_grad


def solution(mesh):
    return jax.shard_map(
        on_device,
        mesh=mesh,
        in_specs=(
            P(("groups", "band", "col"), None),
            P(("groups", "band", "col"), None),
            P(("groups", "band", "col"), None),
            P(("groups", "band", "col"), None),
            P("groups"),
            P("groups"),
            P("groups"),
        ),
        out_specs=(P(("groups", "band", "col"), None), P(("groups", "band", "col"), None)),
        check_vma=False,
    )
```
